32 devices in a mesh: layer: 2 (over y), tensor: 8 (over z, x), dp: 2 (over core).
Axes of the slice: x: 2, y: 2, z: 4, core: 2. Of those that a mesh axis runs over, the one named last changes fastest.
Arguments:
- resid_in: bfloat16 [2, 512, 4096], P('layer', 'dp', 'tensor'), may hold values from -6 to 6
- w_enc: bfloat16 [2, 4096, 4096], P('layer', 'dp', 'tensor'), may hold values from -0.09375 to 0.09375
- threshold: float32 [2, 4096], P('layer', 'tensor'), may hold values from 0.05 to 1
- block_mask: int32 [2, 4, 32], P('layer', 'dp', 'tensor'), may hold values 0 or 1
- w_dec: bfloat16 [2, 4096, 4096], P('layer', 'tensor', 'dp'), may hold values from -0.125 to 0.125
- w_cross: bfloat16 [4096, 4096], P('tensor', 'dp'), may hold values from -0.125 to 0.125
Outputs:
- recon: bfloat16 [2, 512, 4096], P('layer', 'dp', 'tensor')
The draws below stay inside these ranges and needn't reach their ends.
All inputs are finite; a program needn't handle non-finite values. No bound on the sum of `block_mask` on one device may be relied on, other than what follows from the above.
Results may differ from the reference program's by a relative error of at most 0.0049.
Values may be sent and summed in bfloat16 or wider, within the bound.
A program may use at most 64 MiB of HBM per device.

```python
import math
import jax
import jax.numpy as jnp

D = 4096
TILE = 128
BLOCK = 128
LAYERS = 2
LAT = 4096
ROWS = 512


def touch_ends(result, rng, low, top_value):
    longest = result.shape.index(max(result.shape))
    spots = []
    for shift in (0, 1):
        where = [jax.random.randint(jax.random.fold_in(rng, axis), (), 0, length) for axis, length in enumerate(result.shape)]
        where[longest] = (where[longest] + shift) % result.shape[longest]
        spots.append(tuple(where))
    return result.at[spots[0]].set(low).at[spots[1]].set(top_value)


def with_spikes(array, own_key, source, target, shards_of, factor):
    def block_of(dim):
        return (jnp.arange(array.shape[dim]) // (array.shape[dim] // shards_of)).reshape((-1,) + (1,) * (array.ndim - 1 - dim))

    first = jax.random.permutation(own_key, shards_of)[block_of(target)]
    second = (block_of(target) + shards_of // 2) % shards_of
    return jnp.where((block_of(source) == first) | (block_of(source) == second), factor * array, array)


def levels(rng, extent, split, low, high):
    level, own = 1.0, jax.random.fold_in(rng, 6)
    for axis_at, parts in split:
        draws = jnp.exp(jax.random.uniform(jax.random.fold_in(own, axis_at), (parts,), jnp.float32, low / len(split), high / len(split)))
        level = level * jnp.repeat(draws, extent[axis_at] // parts).reshape([-1 if axis == axis_at else 1 for axis in range(len(extent))])
    return level


def normal_values(own_key, dims, spread, most, cuts=(), held_as=jnp.bfloat16):
    level = levels(own_key, dims, cuts, -0.22, 0.18) if cuts else 1.0
    drawn = jax.random.normal(own_key, dims, jnp.float32) * spread * level
    return jnp.minimum(jnp.maximum(drawn, -most), most).astype(held_as)


def noise_with(own_key, dims, scale, limit, shards, heavy, held_as=jnp.bfloat16):
    entries = scale * jax.random.normal(own_key, dims, jnp.float32)
    if shards:
        entries = entries * levels(own_key, dims, shards, -0.22, 0.18)
    return jnp.clip(with_spikes(entries, jax.random.fold_in(own_key, 3), *heavy), -limit, limit).astype(held_as)


def setup_inputs(seed: int = 0) -> dict:
    key_of = jax.random.split(jax.random.key(seed), 7)
    resid_in = normal_values(key_of[0], (LAYERS, ROWS, D), 1.0, 6.0, ((0, 2), (1, 2), (2, 8)))
    w_enc = normal_values(key_of[1], (LAYERS, D, LAT), D ** -0.5, 0.09375, ((0, 2), (1, 2), (2, 8)))
    threshold = jnp.clip(jnp.exp(math.log(1.0) - 2.9957323 * jax.random.uniform(key_of[2], (LAYERS, LAT), jnp.float32) ** levels(key_of[2], (LAYERS, LAT), ((0, 2), (1, 8)), -0.2, 0.2)), 0.05, 1.0)
    block_mask = touch_ends((jax.random.randint(key_of[3], (LAYERS, ROWS // TILE, LAT // BLOCK), 0, 4) < 3).astype(jnp.int32), jax.random.fold_in(key_of[3], 1), 0, 1)
    w_dec = noise_with(key_of[4], (LAYERS, LAT, D), LAT ** -0.5, 0.125, ((0, 2), (1, 8), (2, 2)), (1, 2, 8, 2.0))
    w_cross = noise_with(key_of[5], (LAT, D), LAT ** -0.5, 0.125, ((0, 8), (1, 2)), (0, 1, 8, 2.0))
    return {"resid_in": resid_in, "w_enc": w_enc, "threshold": threshold, "block_mask": block_mask, "w_dec": w_dec, "w_cross": w_cross}


def gate_codes(preact, thresh, activity):
    tile_count, block_count = activity.shape
    shaped = preact.reshape(tile_count, TILE, block_count, BLOCK)
    limits = thresh.reshape(1, 1, block_count, BLOCK)
    gating = activity.astype(preact.dtype)[:, None, :, None]
    active = jnp.maximum(shaped - limits, 0.0) * gating
    return active.reshape(preact.shape).astype(jnp.bfloat16)


def reference(resid_in, w_enc, threshold, block_mask, w_dec, w_cross):
    early_codes = gate_codes(jnp.dot(resid_in[0], w_enc[0], preferred_element_type=jnp.float32), threshold[0], block_mask[0])
    late_codes = gate_codes(jnp.dot(resid_in[1], w_enc[1], preferred_element_type=jnp.float32), threshold[1], block_mask[1])
    recon_early = jnp.dot(early_codes, w_dec[0], preferred_element_type=jnp.float32)
    recon_late = jnp.dot(late_codes, w_dec[1], preferred_element_type=jnp.float32) + jnp.dot(early_codes, w_cross, preferred_element_type=jnp.float32)
    return jnp.stack([recon_early, recon_late]).astype(jnp.bfloat16)
```

```python
import functools

import jax
import jax.numpy as jnp
from jax import lax
from jax.experimental import pallas as pl
from jax.experimental.pallas import tpu as pltpu
from jax.sharding import PartitionSpec as P

TILE = 128
BLOCK = 128
CHUNKS = 2
GATHER_LAG = 0
SUM_LAG = 0


def grid_of(count):
    inner = 1
    while (inner * 2) ** 2 <= count:
        inner *= 2
    return count // inner, inner


def far_first(outer):
    return [sorted(range(outer), key=lambda to: (-abs(to - at), -to if at < outer / 2 else to)) for at in range(outer)]


def kernel(
    sizes, resid, thresh, mask, w_enc, w_dec, w_cross, out,
    feat, enc_buf, dec_buf, cross_buf, codes, early, held, own, x_out, x_in, z_out, up_in, down_in,
    local_sem, w_send, w_recv, g_recv, g_zsend, g_xsend, c_send, c_recv, x_send, x_recv, z_send, up_recv, down_recv,
):
    outer, inner, dp_count = sizes
    count = outer * inner
    per_slab = count // dp_count
    part_rows, part_cols = feat.shape[2:]
    layer = lax.axis_index("layer")
    me = lax.axis_index("tensor")
    dp = lax.axis_index("dp")
    z, x = me // inner, me % inner

    def to_tensor(index):
        return {"tensor": index}

    def x_peer(step):
        return lax.rem(x + step, inner)

    def dp_peer(step):
        return {"dp": lax.rem(dp + step, dp_count)}

    other_layer = {"layer": 1 - layer}
    above, below = me + inner, me - inner
    has_above, has_below = z < outer - 1, z > 0

    weights = ((w_enc, enc_buf), (w_dec, dec_buf), (w_cross, cross_buf))

    def local_copy(which):
        source, target = weights[which]
        return pltpu.make_async_copy(source, target.at[dp], local_sem.at[which])

    def weight_copy(which, step):
        source, target = weights[which]
        return pltpu.make_async_remote_copy(
            source, target.at[dp], w_send.at[which, step - 1], w_recv.at[which, step - 1],
            device_id=dp_peer(step), device_id_type=pl.DeviceIdType.MESH,
        )

    def weight_arrival(which, step):
        source, target = weights[which]
        index = lax.rem(dp + dp_count - step, dp_count)
        return pltpu.make_async_remote_copy(
            source, target.at[index], w_send.at[which, step - 1], w_recv.at[which, step - 1],
            device_id=dp_peer(step), device_id_type=pl.DeviceIdType.MESH,
        )

    def when_used(which, act):
        if which == 2:
            pl.when(layer == 1)(act)
        else:
            act()

    for which in range(3):
        when_used(which, lambda which=which: local_copy(which).start())

    barrier = pltpu.get_barrier_semaphore()

    def greet(where):
        pl.semaphore_signal(barrier, inc=1, device_id=where, device_id_type=pl.DeviceIdType.MESH)

    for step in range(1, inner):
        greet(to_tensor(z * inner + x_peer(step)))
    for step in range(1, dp_count):
        greet(dp_peer(step))
    greet(other_layer)
    pl.when(has_above)(lambda: greet(to_tensor(above)))
    pl.when(has_below)(lambda: greet(to_tensor(below)))
    ends = (z + outer - 1) // outer + (2 * outer - 2 - z) // outer
    pl.semaphore_wait(barrier, inner - 1 + dp_count - 1 + 1 + ends)

    def rows_of(chunk):
        return pl.ds(chunk * part_rows, part_rows)

    def gather_copy(chunk, line, send_sem, where, is_own):
        index = line * inner + x
        return pltpu.make_async_remote_copy(
            resid.at[0, rows_of(chunk)] if is_own else feat.at[chunk, index], feat.at[chunk, index],
            send_sem, g_recv.at[chunk, index], device_id=to_tensor(where), device_id_type=pl.DeviceIdType.MESH,
        )

    def gather_arrival(chunk, index):
        slot = feat.at[chunk, index]
        return pltpu.make_async_remote_copy(
            slot, slot, g_zsend.at[chunk, 0, 0], g_recv.at[chunk, index],
            device_id=other_layer, device_id_type=pl.DeviceIdType.MESH,
        )

    def pass_on(chunk, distance, finish):
        is_own = distance == 0

        def act(copy):
            if finish:
                copy.wait_send()
            else:
                copy.start()

        def to_inner(line):
            for step in range(1, inner):
                act(gather_copy(chunk, line, g_xsend.at[chunk, line, step - 1], z * inner + x_peer(step), is_own))

        def upward(line):
            act(gather_copy(chunk, line, g_zsend.at[chunk, line, 0], above, is_own))

        def downward(line):
            act(gather_copy(chunk, line, g_zsend.at[chunk, line, 1], below, is_own))

        if is_own:
            pl.when(has_above)(lambda: upward(z))
            pl.when(has_below)(lambda: downward(z))
            to_inner(z)
            return

        @pl.when(z >= distance)
        def _():
            line = z - distance
            if not finish:
                gather_arrival(chunk, line * inner + x).wait_recv()
            pl.when(has_above)(lambda: upward(line))
            to_inner(line)

        @pl.when(z < outer - distance)
        def _():
            line = z + distance
            if not finish:
                gather_arrival(chunk, line * inner + x).wait_recv()
            pl.when(has_below)(lambda: downward(line))
            to_inner(line)

    steps = sorted(((c, s) for c in range(CHUNKS) for s in range(outer)), key=lambda cs: (cs[1] + GATHER_LAG * cs[0], cs[0]))
    opening = [cs for cs in steps if cs[1] == 0]
    for chunk, distance in opening:
        pass_on(chunk, distance, False)
    for which in range(3):
        for step in range(1, dp_count):
            when_used(which, lambda which=which, step=step: weight_copy(which, step).start())
    for chunk in range(CHUNKS):
        feat[chunk, me] = resid[0, chunk * part_rows:(chunk + 1) * part_rows, :]
    for chunk, distance in steps:
        if distance:
            pass_on(chunk, distance, False)

    def weights_ready(which):
        local_copy(which).wait()
        for step in range(1, dp_count):
            weight_arrival(which, step).wait_recv()

    def codes_copy(chunk):
        return pltpu.make_async_remote_copy(
            codes.at[chunk], early.at[chunk], c_send.at[chunk], c_recv.at[chunk],
            device_id=other_layer, device_id_type=pl.DeviceIdType.MESH,
        )

    def encode(chunk):
        for line in range(outer):
            for step in range(1, inner):
                gather_arrival(chunk, line * inner + x_peer(step)).wait_recv()
        total = None
        for index in range(count):
            at = (index % per_slab) * part_cols
            term = jnp.dot(
                feat[chunk, index], enc_buf[index // per_slab, at:at + part_cols, :], preferred_element_type=jnp.float32
            )
            total = term if total is None else total + term
        active = jnp.maximum(total - thresh[...], 0.0)
        tile = chunk * part_rows // TILE
        for block in range(active.shape[1] // BLOCK):
            gate = mask[0, tile, block].astype(jnp.float32)
            at = block * BLOCK
            codes[chunk, :, at:at + BLOCK] = (active[:, at:at + BLOCK] * gate).astype(jnp.bfloat16)
        pl.when(layer == 0)(lambda: codes_copy(chunk).start())

    order = far_first(outer)

    def nth(place):
        value = order[0][place]
        for at in range(1, outer):
            value = jnp.where(z == at, order[at][place], value)
        return value

    def share(chunk, index, target):
        slab = index // per_slab
        columns = pl.ds(pl.multiple_of((index % per_slab) * part_cols, part_cols), part_cols)
        target[...] = jnp.dot(codes[chunk], dec_buf[slab, :, columns], preferred_element_type=jnp.float32)

        @pl.when(layer == 1)
        def _():
            target[...] += jnp.dot(early[chunk], cross_buf[slab, :, columns], preferred_element_type=jnp.float32)

    def x_copy(chunk, step, line):
        return pltpu.make_async_remote_copy(
            x_out.at[chunk, step - 1, line], x_in.at[chunk, step - 1, line],
            x_send.at[chunk, step - 1, line], x_recv.at[chunk, step - 1, line],
            device_id=to_tensor(z * inner + x_peer(step)), device_id_type=pl.DeviceIdType.MESH,
        )

    def decode(chunk):
        pl.when(layer == 1)(lambda: codes_copy(chunk).wait_recv())
        for place in range(outer):
            line = nth(place)
            for step in range(1, inner):
                share(chunk, line * inner + x_peer(step), held)
                x_out[chunk, step - 1, line] = held[...].astype(jnp.bfloat16)
                x_copy(chunk, step, line).start()
        for place in range(outer):
            line = nth(place)
            share(chunk, line * inner + x, own.at[chunk, line])

    def up_copy(chunk, line):
        return pltpu.make_async_remote_copy(
            z_out.at[chunk, line], up_in.at[chunk, line], z_send.at[chunk, line], up_recv.at[chunk, line],
            device_id=to_tensor(above), device_id_type=pl.DeviceIdType.MESH,
        )

    def down_copy(chunk, line):
        return pltpu.make_async_remote_copy(
            z_out.at[chunk, line], down_in.at[chunk, line], z_send.at[chunk, line], down_recv.at[chunk, line],
            device_id=to_tensor(below), device_id_type=pl.DeviceIdType.MESH,
        )

    def add_up(chunk, place):
        line = nth(place)
        total = own.at[chunk, line]
        for step in range(1, inner):
            x_copy(chunk, step, line).wait_recv()
            total[...] += x_in[chunk, step - 1, line].astype(jnp.float32)

        def from_below():
            up_copy(chunk, line).wait_recv()
            total[...] += up_in[chunk, line].astype(jnp.float32)

        def from_above():
            down_copy(chunk, line).wait_recv()
            total[...] += down_in[chunk, line].astype(jnp.float32)

        if place == outer - 1:
            pl.when(has_below)(from_below)
            pl.when(has_above)(from_above)
            out[0, chunk * part_rows:(chunk + 1) * part_rows, :] = total[...].astype(jnp.bfloat16)
            return

        @pl.when(line > z)
        def _():
            pl.when(has_below)(from_below)
            z_out[chunk, line] = total[...].astype(jnp.bfloat16)
            up_copy(chunk, line).start()

        @pl.when(line < z)
        def _():
            pl.when(has_above)(from_above)
            z_out[chunk, line] = total[...].astype(jnp.bfloat16)
            down_copy(chunk, line).start()

    weights_ready(0)
    for chunk in range(CHUNKS):
        encode(chunk)
    weights_ready(1)
    pl.when(layer == 1)(lambda: weights_ready(2))
    for chunk in range(CHUNKS):
        decode(chunk)
    sums = sorted(((c, k) for c in range(CHUNKS) for k in range(outer)), key=lambda ck: (ck[1] + SUM_LAG * ck[0], ck[0]))
    for chunk, place in sums:
        add_up(chunk, place)

    for chunk, distance in steps:
        pass_on(chunk, distance, True)
    for which in range(3):
        for step in range(1, dp_count):
            when_used(which, lambda which=which, step=step: weight_copy(which, step).wait_send())
    for chunk in range(CHUNKS):
        pl.when(layer == 0)(lambda chunk=chunk: codes_copy(chunk).wait_send())
        for line in range(outer):
            for step in range(1, inner):
                x_copy(chunk, step, line).wait_send()
            pl.when(line > z)(lambda chunk=chunk, line=line: up_copy(chunk, line).wait_send())
            pl.when(line < z)(lambda chunk=chunk, line=line: down_copy(chunk, line).wait_send())


def shards(mesh_shape, resid_in, w_enc, threshold, block_mask, w_dec, w_cross):
    count, dp_count = mesh_shape["tensor"], mesh_shape["dp"]
    outer, inner = grid_of(count)
    _, rows, cols = resid_in.shape
    part = rows // CHUNKS
    latents = w_enc.shape[2]
    deep, wide = w_enc.shape[1], w_dec.shape[2]
    bf16, f32 = jnp.bfloat16, jnp.float32
    dma = pltpu.SemaphoreType.DMA
    vmem = pl.BlockSpec(memory_space=pltpu.VMEM)
    anywhere = pl.BlockSpec(memory_space=pl.ANY)
    return pl.pallas_call(
        functools.partial(kernel, (outer, inner, dp_count)),
        out_shape=jax.ShapeDtypeStruct((1, rows, cols), bf16),
        in_specs=[vmem, vmem, pl.BlockSpec(memory_space=pltpu.SMEM), anywhere, anywhere, anywhere],
        out_specs=vmem,
        scratch_shapes=[
            pltpu.VMEM((CHUNKS, count, part, cols), bf16),
            pltpu.VMEM((dp_count, deep, latents), bf16),
            pltpu.VMEM((dp_count, latents, wide), bf16),
            pltpu.VMEM((dp_count, latents, wide), bf16),
            pltpu.VMEM((CHUNKS, part, latents), bf16),
            pltpu.VMEM((CHUNKS, part, latents), bf16),
            pltpu.VMEM((part, cols), f32),
            pltpu.VMEM((CHUNKS, outer, part, cols), f32),
            pltpu.VMEM((CHUNKS, inner - 1, outer, part, cols), bf16),
            pltpu.VMEM((CHUNKS, inner - 1, outer, part, cols), bf16),
            pltpu.VMEM((CHUNKS, outer, part, cols), bf16),
            pltpu.VMEM((CHUNKS, outer, part, cols), bf16),
            pltpu.VMEM((CHUNKS, outer, part, cols), bf16),
            dma((3,)),
            dma((3, dp_count - 1)),
            dma((3, dp_count - 1)),
            dma((CHUNKS, count)),
            dma((CHUNKS, outer, 2)),
            dma((CHUNKS, outer, inner - 1)),
            dma((CHUNKS,)),
            dma((CHUNKS,)),
            dma((CHUNKS, inner - 1, outer)),
            dma((CHUNKS, inner - 1, outer)),
            dma((CHUNKS, outer)),
            dma((CHUNKS, outer)),
            dma((CHUNKS, outer)),
        ],
        compiler_params=pltpu.CompilerParams(
            collective_id=0, has_side_effects=True, vmem_limit_bytes=48 * 1024 * 1024
        ),
        cost_estimate=pl.CostEstimate(
            flops=6 * rows * latents * cols * count, bytes_accessed=6 * deep * latents * dp_count, transcendentals=0
        ),
    )(resid_in, threshold, block_mask, w_enc[0], w_dec[0], w_cross)


def solution(mesh):
    return jax.shard_map(
        functools.partial(shards, dict(mesh.shape)),
        mesh=mesh,
        in_specs=(
            P("layer", "dp", "tensor"),
            P("layer", "dp", "tensor"),
            P("layer", "tensor"),
            P("layer", "dp", "tensor"),
            P("layer", "tensor", "dp"),
            P("tensor", "dp"),
        ),
        out_specs=P("layer", "dp", "tensor"),
        check_vma=False,
    )
```

```python
import functools

import jax
import jax.numpy as jnp
from jax import lax
from jax.experimental import pallas as pl
from jax.experimental.pallas import tpu as pltpu
from jax.sharding import PartitionSpec as P

TILE = 128
BLOCK = 128
CHUNKS = 2
GATHER_LAG = 0
SUM_LAG = 0
AHEAD = 3


def grid_of(count):
    inner = 1
    while (inner * 2) ** 2 <= count:
        inner *= 2
    return count // inner, inner


def far_first(outer):
    return [sorted(range(outer), key=lambda to: (-abs(to - at), -to if at < outer / 2 else to)) for at in range(outer)]


def kernel(
    sizes, resid, thresh, mask, w_enc, w_dec, w_cross, out,
    limits, gates, feat, enc_buf, dec_buf, cross_buf, codes, early, held, own, x_out, x_in, z_out, up_in, down_in,
    small_sem, feat_sem, local_sem, w_send, w_recv, g_recv, g_zsend, g_xsend, c_send, c_recv, x_send, x_recv, z_send, up_recv, down_recv,
):
    outer, inner, dp_count = sizes
    count = outer * inner
    per_slab = count // dp_count
    part_rows, part_cols = feat.shape[2:]
    layer = lax.axis_index("layer")
    me = lax.axis_index("tensor")
    dp = lax.axis_index("dp")
    z, x = me // inner, me % inner

    def to_tensor(index):
        return {"tensor": index}

    def x_peer(step):
        return lax.rem(x + step, inner)

    def dp_peer(step):
        return {"dp": lax.rem(dp + step, dp_count)}

    other_layer = {"layer": 1 - layer}
    above, below = me + inner, me - inner
    has_above, has_below = z < outer - 1, z > 0

    weights = ((w_enc, enc_buf), (w_dec, dec_buf), (w_cross, cross_buf))

    def local_copy(which):
        source, target = weights[which]
        return pltpu.make_async_copy(source, target.at[dp], local_sem.at[which])

    def weight_copy(which, step):
        source, target = weights[which]
        return pltpu.make_async_remote_copy(
            source, target.at[dp], w_send.at[which, step - 1], w_recv.at[which, step - 1],
            device_id=dp_peer(step), device_id_type=pl.DeviceIdType.MESH,
        )

    def weight_arrival(which, step):
        source, target = weights[which]
        index = lax.rem(dp + dp_count - step, dp_count)
        return pltpu.make_async_remote_copy(
            source, target.at[index], w_send.at[which, step - 1], w_recv.at[which, step - 1],
            device_id=dp_peer(step), device_id_type=pl.DeviceIdType.MESH,
        )

    def when_used(which, act):
        if which == 2:
            pl.when(layer == 1)(act)
        else:
            act()

    limit_copy = pltpu.make_async_copy(thresh, limits, small_sem.at[0])
    gate_copy = pltpu.make_async_copy(mask, gates, small_sem.at[1])

    def own_copy(chunk):
        return pltpu.make_async_copy(
            resid.at[0, pl.ds(chunk * part_rows, part_rows)], feat.at[chunk, me], feat_sem.at[chunk]
        )

    barrier = pltpu.get_barrier_semaphore()

    def greet(where):
        pl.semaphore_signal(barrier, inc=1, device_id=where, device_id_type=pl.DeviceIdType.MESH)

    for step in range(1, inner):
        greet(to_tensor(z * inner + x_peer(step)))
    for step in range(1, dp_count):
        greet(dp_peer(step))
    greet(other_layer)
    pl.when(has_above)(lambda: greet(to_tensor(above)))
    pl.when(has_below)(lambda: greet(to_tensor(below)))
    ends = (z + outer - 1) // outer + (2 * outer - 2 - z) // outer
    pl.semaphore_wait(barrier, inner - 1 + dp_count - 1 + 1 + ends)

    def rows_of(chunk):
        return pl.ds(chunk * part_rows, part_rows)

    def gather_copy(chunk, line, send_sem, where, is_own):
        index = line * inner + x
        return pltpu.make_async_remote_copy(
            resid.at[0, rows_of(chunk)] if is_own else feat.at[chunk, index], feat.at[chunk, index],
            send_sem, g_recv.at[chunk, index], device_id=to_tensor(where), device_id_type=pl.DeviceIdType.MESH,
        )

    def gather_arrival(chunk, index):
        slot = feat.at[chunk, index]
        return pltpu.make_async_remote_copy(
            slot, slot, g_zsend.at[chunk, 0, 0], g_recv.at[chunk, index],
            device_id=other_layer, device_id_type=pl.DeviceIdType.MESH,
        )

    def pass_on(chunk, distance, finish):
        is_own = distance == 0

        def act(copy):
            if finish:
                copy.wait_send()
            else:
                copy.start()

        def to_inner(line):
            for step in range(1, inner):
                act(gather_copy(chunk, line, g_xsend.at[chunk, line, step - 1], z * inner + x_peer(step), is_own))

        def upward(line):
            act(gather_copy(chunk, line, g_zsend.at[chunk, line, 0], above, is_own))

        def downward(line):
            act(gather_copy(chunk, line, g_zsend.at[chunk, line, 1], below, is_own))

        if is_own:
            pl.when(has_above)(lambda: upward(z))
            pl.when(has_below)(lambda: downward(z))
            to_inner(z)
            return

        @pl.when(z >= distance)
        def _():
            line = z - distance
            if not finish:
                gather_arrival(chunk, line * inner + x).wait_recv()
            pl.when(has_above)(lambda: upward(line))
            to_inner(line)

        @pl.when(z < outer - distance)
        def _():
            line = z + distance
            if not finish:
                gather_arrival(chunk, line * inner + x).wait_recv()
            pl.when(has_below)(lambda: downward(line))
            to_inner(line)

    steps = sorted(((c, s) for c in range(CHUNKS) for s in range(outer)), key=lambda cs: (cs[1] + GATHER_LAG * cs[0], cs[0]))
    opening = [cs for cs in steps if cs[1] == 0]
    for chunk, distance in opening:
        pass_on(chunk, distance, False)
    for which in range(3):
        for step in range(1, dp_count):
            when_used(which, lambda which=which, step=step: weight_copy(which, step).start())
    for chunk in range(CHUNKS):
        own_copy(chunk).start()
    limit_copy.start()
    gate_copy.start()
    for which in range(3):
        when_used(which, lambda which=which: local_copy(which).start())
    for chunk, distance in steps:
        if distance:
            pass_on(chunk, distance, False)

    def weights_ready(which):
        local_copy(which).wait()
        for step in range(1, dp_count):
            weight_arrival(which, step).wait_recv()

    def codes_copy(chunk):
        return pltpu.make_async_remote_copy(
            codes.at[chunk], early.at[chunk], c_send.at[chunk], c_recv.at[chunk],
            device_id=other_layer, device_id_type=pl.DeviceIdType.MESH,
        )

    def encode(chunk):
        for line in range(outer):
            for step in range(1, inner):
                gather_arrival(chunk, line * inner + x_peer(step)).wait_recv()
        own_copy(chunk).wait()
        total = None
        for index in range(count):
            at = (index % per_slab) * part_cols
            term = jnp.dot(
                feat[chunk, index], enc_buf[index // per_slab, at:at + part_cols, :], preferred_element_type=jnp.float32
            )
            total = term if total is None else total + term
        active = jnp.maximum(total - limits[...], 0.0)
        tile = chunk * part_rows // TILE
        for block in range(active.shape[1] // BLOCK):
            gate = gates[0, tile:tile + 1, block:block + 1].astype(jnp.float32)
            at = block * BLOCK
            codes[chunk, :, at:at + BLOCK] = (active[:, at:at + BLOCK] * gate).astype(jnp.bfloat16)
        pl.when(layer == 0)(lambda: codes_copy(chunk).start())

    order = far_first(outer)

    def nth(place):
        value = order[0][place]
        for at in range(1, outer):
            value = jnp.where(z == at, order[at][place], value)
        return value

    def share(chunk, index, target):
        slab = index // per_slab
        columns = pl.ds(pl.multiple_of((index % per_slab) * part_cols, part_cols), part_cols)
        target[...] = jnp.dot(codes[chunk], dec_buf[slab, :, columns], preferred_element_type=jnp.float32)

        @pl.when(layer == 1)
        def _():
            target[...] += jnp.dot(early[chunk], cross_buf[slab, :, columns], preferred_element_type=jnp.float32)

    def x_copy(chunk, step, line):
        return pltpu.make_async_remote_copy(
            x_out.at[chunk, step - 1, line], x_in.at[chunk, step - 1, line],
            x_send.at[chunk, step - 1, line], x_recv.at[chunk, step - 1, line],
            device_id=to_tensor(z * inner + x_peer(step)), device_id_type=pl.DeviceIdType.MESH,
        )

    def exchange(chunk, place):
        line = nth(place)
        for step in range(1, inner):
            share(chunk, line * inner + x_peer(step), held)
            x_out[chunk, step - 1, line] = held[...].astype(jnp.bfloat16)
            x_copy(chunk, step, line).start()
        share(chunk, line * inner + x, own.at[chunk, line])

    def up_copy(chunk, line):
        return pltpu.make_async_remote_copy(
            z_out.at[chunk, line], up_in.at[chunk, line], z_send.at[chunk, line], up_recv.at[chunk, line],
            device_id=to_tensor(above), device_id_type=pl.DeviceIdType.MESH,
        )

    def down_copy(chunk, line):
        return pltpu.make_async_remote_copy(
            z_out.at[chunk, line], down_in.at[chunk, line], z_send.at[chunk, line], down_recv.at[chunk, line],
            device_id=to_tensor(below), device_id_type=pl.DeviceIdType.MESH,
        )

    def add_up(chunk, place):
        line = nth(place)
        total = own.at[chunk, line]
        for step in range(1, inner):
            x_copy(chunk, step, line).wait_recv()
            total[...] += x_in[chunk, step - 1, line].astype(jnp.float32)

        def from_below():
            up_copy(chunk, line).wait_recv()
            total[...] += up_in[chunk, line].astype(jnp.float32)

        def from_above():
            down_copy(chunk, line).wait_recv()
            total[...] += down_in[chunk, line].astype(jnp.float32)

        if place == outer - 1:
            pl.when(has_below)(from_below)
            pl.when(has_above)(from_above)
            out[0, chunk * part_rows:(chunk + 1) * part_rows, :] = total[...].astype(jnp.bfloat16)
            return

        @pl.when(line > z)
        def _():
            pl.when(has_below)(from_below)
            z_out[chunk, line] = total[...].astype(jnp.bfloat16)
            up_copy(chunk, line).start()

        @pl.when(line < z)
        def _():
            pl.when(has_above)(from_above)
            z_out[chunk, line] = total[...].astype(jnp.bfloat16)
            down_copy(chunk, line).start()

    limit_copy.wait()
    gate_copy.wait()
    weights_ready(0)
    for chunk in range(CHUNKS):
        encode(chunk)
    weights_ready(1)
    pl.when(layer == 1)(lambda: weights_ready(2))
    for chunk in range(CHUNKS):
        pl.when(layer == 1)(lambda chunk=chunk: codes_copy(chunk).wait_recv())
    sums = sorted(((c, k) for c in range(CHUNKS) for k in range(outer)), key=lambda ck: (ck[1] + SUM_LAG * ck[0], ck[0]))
    for at, item in enumerate(sums):
        exchange(*item)
        if at >= AHEAD:
            add_up(*sums[at - AHEAD])
    for item in sums[len(sums) - AHEAD:]:
        add_up(*item)

    for chunk, distance in steps:
        pass_on(chunk, distance, True)
    for which in range(3):
        for step in range(1, dp_count):
            when_used(which, lambda which=which, step=step: weight_copy(which, step).wait_send())
    for chunk in range(CHUNKS):
        pl.when(layer == 0)(lambda chunk=chunk: codes_copy(chunk).wait_send())
        for line in range(outer):
            for step in range(1, inner):
                x_copy(chunk, step, line).wait_send()
            pl.when(line > z)(lambda chunk=chunk, line=line: up_copy(chunk, line).wait_send())
            pl.when(line < z)(lambda chunk=chunk, line=line: down_copy(chunk, line).wait_send())


def shards(mesh_shape, resid_in, w_enc, threshold, block_mask, w_dec, w_cross):
    count, dp_count = mesh_shape["tensor"], mesh_shape["dp"]
    outer, inner = grid_of(count)
    _, rows, cols = resid_in.shape
    part = rows // CHUNKS
    latents = w_enc.shape[2]
    deep, wide = w_enc.shape[1], w_dec.shape[2]
    bf16, f32 = jnp.bfloat16, jnp.float32
    dma = pltpu.SemaphoreType.DMA
    vmem = pl.BlockSpec(memory_space=pltpu.VMEM)
    hbm = pl.BlockSpec(memory_space=pltpu.HBM)
    return pl.pallas_call(
        functools.partial(kernel, (outer, inner, dp_count)),
        out_shape=jax.ShapeDtypeStruct((1, rows, cols), bf16),
        in_specs=[hbm] * 6,
        out_specs=vmem,
        scratch_shapes=[
            pltpu.VMEM((1, latents), f32),
            pltpu.VMEM(block_mask.shape, jnp.int32),
            pltpu.VMEM((CHUNKS, count, part, cols), bf16),
            pltpu.VMEM((dp_count, deep, latents), bf16),
            pltpu.VMEM((dp_count, latents, wide), bf16),
            pltpu.VMEM((dp_count, latents, wide), bf16),
            pltpu.VMEM((CHUNKS, part, latents), bf16),
            pltpu.VMEM((CHUNKS, part, latents), bf16),
            pltpu.VMEM((part, cols), f32),
            pltpu.VMEM((CHUNKS, outer, part, cols), f32),
            pltpu.VMEM((CHUNKS, inner - 1, outer, part, cols), bf16),
            pltpu.VMEM((CHUNKS, inner - 1, outer, part, cols), bf16),
            pltpu.VMEM((CHUNKS, outer, part, cols), bf16),
            pltpu.VMEM((CHUNKS, outer, part, cols), bf16),
            pltpu.VMEM((CHUNKS, outer, part, cols), bf16),
            dma((2,)),
            dma((CHUNKS,)),
            dma((3,)),
            dma((3, dp_count - 1)),
            dma((3, dp_count - 1)),
            dma((CHUNKS, count)),
            dma((CHUNKS, outer, 2)),
            dma((CHUNKS, outer, inner - 1)),
            dma((CHUNKS,)),
            dma((CHUNKS,)),
            dma((CHUNKS, inner - 1, outer)),
            dma((CHUNKS, inner - 1, outer)),
            dma((CHUNKS, outer)),
            dma((CHUNKS, outer)),
            dma((CHUNKS, outer)),
        ],
        compiler_params=pltpu.CompilerParams(
            collective_id=0, has_side_effects=True, vmem_limit_bytes=60 * 1024 * 1024
        ),
        cost_estimate=pl.CostEstimate(
            flops=6 * rows * latents * cols * count, bytes_accessed=6 * deep * latents * dp_count, transcendentals=0
        ),
    )(resid_in, threshold, block_mask, w_enc[0], w_dec[0], w_cross)


def solution(mesh):
    return jax.shard_map(
        functools.partial(shards, dict(mesh.shape)),
        mesh=mesh,
        in_specs=(
            P("layer", "dp", "tensor"),
            P("layer", "dp", "tensor"),
            P("layer", "tensor"),
            P("layer", "dp", "tensor"),
            P("layer", "tensor", "dp"),
            P("tensor", "dp"),
        ),
        out_specs=P("layer", "dp", "tensor"),
        check_vma=False,
    )
```

```python
import functools

import jax
import jax.numpy as jnp
from jax import lax
from jax.experimental import pallas as pl
from jax.experimental.pallas import tpu as pltpu
from jax.sharding import PartitionSpec as P

TILE = 128
BLOCK = 128
CHUNKS = 2
GATHER_LAG = 0
SUM_LAG = 0
AHEAD = 4


def grid_of(count):
    inner = 1
    while (inner * 2) ** 2 <= count:
        inner *= 2
    return count // inner, inner


def far_first(outer):
    return [sorted(range(outer), key=lambda to: (-abs(to - at), -to if at < outer / 2 else to)) for at in range(outer)]


def kernel(
    sizes, resid, thresh, mask, w_enc, w_dec, w_cross, out,
    limits, gates, feat, enc_buf, dec_buf, cross_buf, codes, early, held, own, x_out, x_in, z_out, up_in, down_in,
    small_sem, feat_sem, local_sem, w_send, w_recv, g_recv, g_zsend, g_xsend, c_send, c_recv, x_send, x_recv, z_send, up_recv, down_recv,
):
    outer, inner, dp_count = sizes
    count = outer * inner
    per_slab = count // dp_count
    part_rows, part_cols = feat.shape[2:]
    layer = lax.axis_index("layer")
    me = lax.axis_index("tensor")
    dp = lax.axis_index("dp")
    z, x = me // inner, me % inner

    def to_tensor(index):
        return {"tensor": index}

    def x_peer(step):
        return lax.rem(x + step, inner)

    def dp_peer(step):
        return {"dp": lax.rem(dp + step, dp_count)}

    other_layer = {"layer": 1 - layer}
    above, below = me + inner, me - inner
    has_above, has_below = z < outer - 1, z > 0

    weights = ((w_enc, enc_buf), (w_dec, dec_buf), (w_cross, cross_buf))

    def local_copy(which):
        source, target = weights[which]
        return pltpu.make_async_copy(source, target.at[dp], local_sem.at[which])

    def weight_copy(which, step):
        source, target = weights[which]
        return pltpu.make_async_remote_copy(
            source, target.at[dp], w_send.at[which, step - 1], w_recv.at[which, step - 1],
            device_id=dp_peer(step), device_id_type=pl.DeviceIdType.MESH,
        )

    def weight_arrival(which, step):
        source, target = weights[which]
        index = lax.rem(dp + dp_count - step, dp_count)
        return pltpu.make_async_remote_copy(
            source, target.at[index], w_send.at[which, step - 1], w_recv.at[which, step - 1],
            device_id=dp_peer(step), device_id_type=pl.DeviceIdType.MESH,
        )

    def when_used(which, act):
        if which == 2:
            pl.when(layer == 1)(act)
        else:
            act()

    limit_copy = pltpu.make_async_copy(thresh, limits, small_sem.at[0])
    gate_copy = pltpu.make_async_copy(mask, gates, small_sem.at[1])

    def own_copy(chunk):
        return pltpu.make_async_copy(
            resid.at[0, pl.ds(chunk * part_rows, part_rows)], feat.at[chunk, me], feat_sem.at[chunk]
        )

    barrier = pltpu.get_barrier_semaphore()

    def greet(where):
        pl.semaphore_signal(barrier, inc=1, device_id=where, device_id_type=pl.DeviceIdType.MESH)

    for step in range(1, inner):
        greet(to_tensor(z * inner + x_peer(step)))
    for step in range(1, dp_count):
        greet(dp_peer(step))
    greet(other_layer)
    pl.when(has_above)(lambda: greet(to_tensor(above)))
    pl.when(has_below)(lambda: greet(to_tensor(below)))
    ends = (z + outer - 1) // outer + (2 * outer - 2 - z) // outer
    pl.semaphore_wait(barrier, inner - 1 + dp_count - 1 + 1 + ends)

    def rows_of(chunk):
        return pl.ds(chunk * part_rows, part_rows)

    def gather_copy(chunk, line, send_sem, where, is_own):
        index = line * inner + x
        return pltpu.make_async_remote_copy(
            resid.at[0, rows_of(chunk)] if is_own else feat.at[chunk, index], feat.at[chunk, index],
            send_sem, g_recv.at[chunk, index], device_id=to_tensor(where), device_id_type=pl.DeviceIdType.MESH,
        )

    def gather_arrival(chunk, index):
        slot = feat.at[chunk, index]
        return pltpu.make_async_remote_copy(
            slot, slot, g_zsend.at[chunk, 0, 0], g_recv.at[chunk, index],
            device_id=other_layer, device_id_type=pl.DeviceIdType.MESH,
        )

    def pass_on(chunk, distance, finish):
        is_own = distance == 0

        def act(copy):
            if finish:
                copy.wait_send()
            else:
                copy.start()

        def to_inner(line):
            for step in range(1, inner):
                act(gather_copy(chunk, line, g_xsend.at[chunk, line, step - 1], z * inner + x_peer(step), is_own))

        def upward(line):
            act(gather_copy(chunk, line, g_zsend.at[chunk, line, 0], above, is_own))

        def downward(line):
            act(gather_copy(chunk, line, g_zsend.at[chunk, line, 1], below, is_own))

        if is_own:
            pl.when(has_above)(lambda: upward(z))
            pl.when(has_below)(lambda: downward(z))
            to_inner(z)
            return

        @pl.when(z >= distance)
        def _():
            line = z - distance
            if not finish:
                gather_arrival(chunk, line * inner + x).wait_recv()
            pl.when(has_above)(lambda: upward(line))
            to_inner(line)

        @pl.when(z < outer - distance)
        def _():
            line = z + distance
            if not finish:
                gather_arrival(chunk, line * inner + x).wait_recv()
            pl.when(has_below)(lambda: downward(line))
            to_inner(line)

    steps = sorted(((c, s) for c in range(CHUNKS) for s in range(outer)), key=lambda cs: (cs[1] + GATHER_LAG * cs[0], cs[0]))
    opening = [cs for cs in steps if cs[1] == 0]
    for chunk, distance in opening:
        pass_on(chunk, distance, False)
    for which in range(3):
        for step in range(1, dp_count):
            when_used(which, lambda which=which, step=step: weight_copy(which, step).start())
    for chunk in range(CHUNKS):
        own_copy(chunk).start()
    limit_copy.start()
    gate_copy.start()
    for which in range(3):
        when_used(which, lambda which=which: local_copy(which).start())
    for chunk, distance in steps:
        if distance:
            pass_on(chunk, distance, False)

    def weights_ready(which):
        local_copy(which).wait()
        for step in range(1, dp_count):
            weight_arrival(which, step).wait_recv()

    def codes_copy(chunk):
        return pltpu.make_async_remote_copy(
            codes.at[chunk], early.at[chunk], c_send.at[chunk], c_recv.at[chunk],
            device_id=other_layer, device_id_type=pl.DeviceIdType.MESH,
        )

    def encode(chunk):
        for line in range(outer):
            for step in range(1, inner):
                gather_arrival(chunk, line * inner + x_peer(step)).wait_recv()
        own_copy(chunk).wait()
        total = None
        for index in range(count):
            at = (index % per_slab) * part_cols
            term = jnp.dot(
                feat[chunk, index], enc_buf[index // per_slab, at:at + part_cols, :], preferred_element_type=jnp.float32
            )
            total = term if total is None else total + term
        active = jnp.maximum(total - limits[...], 0.0)
        tile = chunk * part_rows // TILE
        for block in range(active.shape[1] // BLOCK):
            gate = gates[0, tile:tile + 1, block:block + 1].astype(jnp.float32)
            at = block * BLOCK
            codes[chunk, :, at:at + BLOCK] = (active[:, at:at + BLOCK] * gate).astype(jnp.bfloat16)
        pl.when(layer == 0)(lambda: codes_copy(chunk).start())

    order = far_first(outer)

    def nth(place):
        value = order[0][place]
        for at in range(1, outer):
            value = jnp.where(z == at, order[at][place], value)
        return value

    def share(chunk, index, target):
        slab = index // per_slab
        columns = pl.ds(pl.multiple_of((index % per_slab) * part_cols, part_cols), part_cols)
        target[...] = jnp.dot(codes[chunk], dec_buf[slab, :, columns], preferred_element_type=jnp.float32)

        @pl.when(layer == 1)
        def _():
            target[...] += jnp.dot(early[chunk], cross_buf[slab, :, columns], preferred_element_type=jnp.float32)

    def x_copy(chunk, step, line):
        return pltpu.make_async_remote_copy(
            x_out.at[chunk, step - 1, line], x_in.at[chunk, step - 1, line],
            x_send.at[chunk, step - 1, line], x_recv.at[chunk, step - 1, line],
            device_id=to_tensor(z * inner + x_peer(step)), device_id_type=pl.DeviceIdType.MESH,
        )

    def exchange(chunk, place):
        line = nth(place)
        for step in range(1, inner):
            share(chunk, line * inner + x_peer(step), held)
            x_out[chunk, step - 1, line] = held[...].astype(jnp.bfloat16)
            x_copy(chunk, step, line).start()
        share(chunk, line * inner + x, own.at[chunk, line])

    def up_copy(chunk, line):
        return pltpu.make_async_remote_copy(
            z_out.at[chunk, line], up_in.at[chunk, line], z_send.at[chunk, line], up_recv.at[chunk, line],
            device_id=to_tensor(above), device_id_type=pl.DeviceIdType.MESH,
        )

    def down_copy(chunk, line):
        return pltpu.make_async_remote_copy(
            z_out.at[chunk, line], down_in.at[chunk, line], z_send.at[chunk, line], down_recv.at[chunk, line],
            device_id=to_tensor(below), device_id_type=pl.DeviceIdType.MESH,
        )

    def add_up(chunk, place):
        line = nth(place)
        total = own.at[chunk, line]
        for step in range(1, inner):
            x_copy(chunk, step, line).wait_recv()
            total[...] += x_in[chunk, step - 1, line].astype(jnp.float32)

        def from_below():
            up_copy(chunk, line).wait_recv()
            total[...] += up_in[chunk, line].astype(jnp.float32)

        def from_above():
            down_copy(chunk, line).wait_recv()
            total[...] += down_in[chunk, line].astype(jnp.float32)

        if place == outer - 1:
            pl.when(has_below)(from_below)
            pl.when(has_above)(from_above)
            out[0, chunk * part_rows:(chunk + 1) * part_rows, :] = total[...].astype(jnp.bfloat16)
            return

        @pl.when(line > z)
        def _():
            pl.when(has_below)(from_below)
            z_out[chunk, line] = total[...].astype(jnp.bfloat16)
            up_copy(chunk, line).start()

        @pl.when(line < z)
        def _():
            pl.when(has_above)(from_above)
            z_out[chunk, line] = total[...].astype(jnp.bfloat16)
            down_copy(chunk, line).start()

    limit_copy.wait()
    gate_copy.wait()
    weights_ready(0)
    for chunk in range(CHUNKS):
        encode(chunk)
    weights_ready(1)
    pl.when(layer == 1)(lambda: weights_ready(2))
    for chunk in range(CHUNKS):
        pl.when(layer == 1)(lambda chunk=chunk: codes_copy(chunk).wait_recv())
    sums = sorted(((c, k) for c in range(CHUNKS) for k in range(outer)), key=lambda ck: (ck[1] + SUM_LAG * ck[0], ck[0]))
    for at, item in enumerate(sums):
        exchange(*item)
        if at >= AHEAD:
            add_up(*sums[at - AHEAD])
    for item in sums[len(sums) - AHEAD:]:
        add_up(*item)

    for chunk, distance in steps:
        pass_on(chunk, distance, True)
    for which in range(3):
        for step in range(1, dp_count):
            when_used(which, lambda which=which, step=step: weight_copy(which, step).wait_send())
    for chunk in range(CHUNKS):
        pl.when(layer == 0)(lambda chunk=chunk: codes_copy(chunk).wait_send())
        for line in range(outer):
            for step in range(1, inner):
                x_copy(chunk, step, line).wait_send()
            pl.when(line > z)(lambda chunk=chunk, line=line: up_copy(chunk, line).wait_send())
            pl.when(line < z)(lambda chunk=chunk, line=line: down_copy(chunk, line).wait_send())


def shards(mesh_shape, resid_in, w_enc, threshold, block_mask, w_dec, w_cross):
    count, dp_count = mesh_shape["tensor"], mesh_shape["dp"]
    outer, inner = grid_of(count)
    _, rows, cols = resid_in.shape
    part = rows // CHUNKS
    latents = w_enc.shape[2]
    deep, wide = w_enc.shape[1], w_dec.shape[2]
    bf16, f32 = jnp.bfloat16, jnp.float32
    dma = pltpu.SemaphoreType.DMA
    vmem = pl.BlockSpec(memory_space=pltpu.VMEM)
    hbm = pl.BlockSpec(memory_space=pltpu.HBM)
    return pl.pallas_call(
        functools.partial(kernel, (outer, inner, dp_count)),
        out_shape=jax.ShapeDtypeStruct((1, rows, cols), bf16),
        in_specs=[hbm] * 6,
        out_specs=vmem,
        scratch_shapes=[
            pltpu.VMEM((1, latents), f32),
            pltpu.VMEM(block_mask.shape, jnp.int32),
            pltpu.VMEM((CHUNKS, count, part, cols), bf16),
            pltpu.VMEM((dp_count, deep, latents), bf16),
            pltpu.VMEM((dp_count, latents, wide), bf16),
            pltpu.VMEM((dp_count, latents, wide), bf16),
            pltpu.VMEM((CHUNKS, part, latents), bf16),
            pltpu.VMEM((CHUNKS, part, latents), bf16),
            pltpu.VMEM((part, cols), f32),
            pltpu.VMEM((CHUNKS, outer, part, cols), f32),
            pltpu.VMEM((CHUNKS, inner - 1, outer, part, cols), bf16),
            pltpu.VMEM((CHUNKS, inner - 1, outer, part, cols), bf16),
            pltpu.VMEM((CHUNKS, outer, part, cols), bf16),
            pltpu.VMEM((CHUNKS, outer, part, cols), bf16),
            pltpu.VMEM((CHUNKS, outer, part, cols), bf16),
            dma((2,)),
            dma((CHUNKS,)),
            dma((3,)),
            dma((3, dp_count - 1)),
            dma((3, dp_count - 1)),
            dma((CHUNKS, count)),
            dma((CHUNKS, outer, 2)),
            dma((CHUNKS, outer, inner - 1)),
            dma((CHUNKS,)),
            dma((CHUNKS,)),
            dma((CHUNKS, inner - 1, outer)),
            dma((CHUNKS, inner - 1, outer)),
            dma((CHUNKS, outer)),
            dma((CHUNKS, outer)),
            dma((CHUNKS, outer)),
        ],
        compiler_params=pltpu.CompilerParams(
            collective_id=0, has_side_effects=True, vmem_limit_bytes=60 * 1024 * 1024
        ),
        cost_estimate=pl.CostEstimate(
            flops=6 * rows * latents * cols * count, bytes_accessed=6 * deep * latents * dp_count, transcendentals=0
        ),
    )(resid_in, threshold, block_mask, w_enc[0], w_dec[0], w_cross)


def solution(mesh):
    return jax.shard_map(
        functools.partial(shards, dict(mesh.shape)),
        mesh=mesh,
        in_specs=(
            P("layer", "dp", "tensor"),
            P("layer", "dp", "tensor"),
            P("layer", "tensor"),
            P("layer", "dp", "tensor"),
            P("layer", "tensor", "dp"),
            P("tensor", "dp"),
        ),
        out_specs=P("layer", "dp", "tensor"),
        check_vma=False,
    )
```

```python
import functools

import jax
import jax.numpy as jnp
from jax import lax
from jax.experimental import pallas as pl
from jax.experimental.pallas import tpu as pltpu
from jax.sharding import PartitionSpec as P

TILE = 128
BLOCK = 128
CHUNKS = 2
GATHER_LAG = 0
SUM_LAG = 0
AHEAD = 5


def grid_of(count):
    inner = 1
    while (inner * 2) ** 2 <= count:
        inner *= 2
    return count // inner, inner


def far_first(outer):
    return [sorted(range(outer), key=lambda to: (-abs(to - at), -to if at < outer / 2 else to)) for at in range(outer)]


def kernel(
    sizes, resid, thresh, mask, w_enc, w_dec, w_cross, out,
    limits, gates, feat, enc_buf, dec_buf, cross_buf, codes, early, held, own, x_out, x_in, z_out, up_in, down_in,
    small_sem, feat_sem, local_sem, w_send, w_recv, g_recv, g_zsend, g_xsend, c_send, c_recv, x_send, x_recv, z_send, up_recv, down_recv,
):
    outer, inner, dp_count = sizes
    count = outer * inner
    per_slab = count // dp_count
    part_rows, part_cols = feat.shape[2:]
    layer = lax.axis_index("layer")
    me = lax.axis_index("tensor")
    dp = lax.axis_index("dp")
    z, x = me // inner, me % inner

    def to_tensor(index):
        return {"tensor": index}

    def x_peer(step):
        return lax.rem(x + step, inner)

    def dp_peer(step):
        return {"dp": lax.rem(dp + step, dp_count)}

    other_layer = {"layer": 1 - layer}
    above, below = me + inner, me - inner
    has_above, has_below = z < outer - 1, z > 0

    weights = ((w_enc, enc_buf), (w_dec, dec_buf), (w_cross, cross_buf))

    def local_copy(which):
        source, target = weights[which]
        return pltpu.make_async_copy(source, target.at[dp], local_sem.at[which])

    def weight_copy(which, step):
        source, target = weights[which]
        return pltpu.make_async_remote_copy(
            source, target.at[dp], w_send.at[which, step - 1], w_recv.at[which, step - 1],
            device_id=dp_peer(step), device_id_type=pl.DeviceIdType.MESH,
        )

    def weight_arrival(which, step):
        source, target = weights[which]
        index = lax.rem(dp + dp_count - step, dp_count)
        return pltpu.make_async_remote_copy(
            source, target.at[index], w_send.at[which, step - 1], w_recv.at[which, step - 1],
            device_id=dp_peer(step), device_id_type=pl.DeviceIdType.MESH,
        )

    def when_used(which, act):
        if which == 2:
            pl.when(layer == 1)(act)
        else:
            act()

    limit_copy = pltpu.make_async_copy(thresh, limits, small_sem.at[0])
    gate_copy = pltpu.make_async_copy(mask, gates, small_sem.at[1])

    def own_copy(chunk):
        return pltpu.make_async_copy(
            resid.at[0, pl.ds(chunk * part_rows, part_rows)], feat.at[chunk, me], feat_sem.at[chunk]
        )

    barrier = pltpu.get_barrier_semaphore()

    def greet(where):
        pl.semaphore_signal(barrier, inc=1, device_id=where, device_id_type=pl.DeviceIdType.MESH)

    for step in range(1, inner):
        greet(to_tensor(z * inner + x_peer(step)))
    for step in range(1, dp_count):
        greet(dp_peer(step))
    greet(other_layer)
    pl.when(has_above)(lambda: greet(to_tensor(above)))
    pl.when(has_below)(lambda: greet(to_tensor(below)))
    ends = (z + outer - 1) // outer + (2 * outer - 2 - z) // outer
    pl.semaphore_wait(barrier, inner - 1 + dp_count - 1 + 1 + ends)

    def rows_of(chunk):
        return pl.ds(chunk * part_rows, part_rows)

    def gather_copy(chunk, line, send_sem, where, is_own):
        index = line * inner + x
        return pltpu.make_async_remote_copy(
            resid.at[0, rows_of(chunk)] if is_own else feat.at[chunk, index], feat.at[chunk, index],
            send_sem, g_recv.at[chunk, index], device_id=to_tensor(where), device_id_type=pl.DeviceIdType.MESH,
        )

    def gather_arrival(chunk, index):
        slot = feat.at[chunk, index]
        return pltpu.make_async_remote_copy(
            slot, slot, g_zsend.at[chunk, 0, 0], g_recv.at[chunk, index],
            device_id=other_layer, device_id_type=pl.DeviceIdType.MESH,
        )

    def pass_on(chunk, distance, finish):
        is_own = distance == 0

        def act(copy):
            if finish:
                copy.wait_send()
            else:
                copy.start()

        def to_inner(line):
            for step in range(1, inner):
                act(gather_copy(chunk, line, g_xsend.at[chunk, line, step - 1], z * inner + x_peer(step), is_own))

        def upward(line):
            act(gather_copy(chunk, line, g_zsend.at[chunk, line, 0], above, is_own))

        def downward(line):
            act(gather_copy(chunk, line, g_zsend.at[chunk, line, 1], below, is_own))

        if is_own:
            pl.when(has_above)(lambda: upward(z))
            pl.when(has_below)(lambda: downward(z))
            to_inner(z)
            return

        @pl.when(z >= distance)
        def _():
            line = z - distance
            if not finish:
                gather_arrival(chunk, line * inner + x).wait_recv()
            pl.when(has_above)(lambda: upward(line))
            to_inner(line)

        @pl.when(z < outer - distance)
        def _():
            line = z + distance
            if not finish:
                gather_arrival(chunk, line * inner + x).wait_recv()
            pl.when(has_below)(lambda: downward(line))
            to_inner(line)

    steps = sorted(((c, s) for c in range(CHUNKS) for s in range(outer)), key=lambda cs: (cs[1] + GATHER_LAG * cs[0], cs[0]))
    opening = [cs for cs in steps if cs[1] == 0]
    for chunk, distance in opening:
        pass_on(chunk, distance, False)
    for which in range(3):
        for step in range(1, dp_count):
            when_used(which, lambda which=which, step=step: weight_copy(which, step).start())
    for chunk in range(CHUNKS):
        own_copy(chunk).start()
    limit_copy.start()
    gate_copy.start()
    for which in range(3):
        when_used(which, lambda which=which: local_copy(which).start())
    for chunk, distance in steps:
        if distance:
            pass_on(chunk, distance, False)

    def weights_ready(which):
        local_copy(which).wait()
        for step in range(1, dp_count):
            weight_arrival(which, step).wait_recv()

    def codes_copy(chunk):
        return pltpu.make_async_remote_copy(
            codes.at[chunk], early.at[chunk], c_send.at[chunk], c_recv.at[chunk],
            device_id=other_layer, device_id_type=pl.DeviceIdType.MESH,
        )

    def encode(chunk):
        for line in range(outer):
            for step in range(1, inner):
                gather_arrival(chunk, line * inner + x_peer(step)).wait_recv()
        own_copy(chunk).wait()
        total = None
        for index in range(count):
            at = (index % per_slab) * part_cols
            term = jnp.dot(
                feat[chunk, index], enc_buf[index // per_slab, at:at + part_cols, :], preferred_element_type=jnp.float32
            )
            total = term if total is None else total + term
        active = jnp.maximum(total - limits[...], 0.0)
        tile = chunk * part_rows // TILE
        for block in range(active.shape[1] // BLOCK):
            gate = gates[0, tile:tile + 1, block:block + 1].astype(jnp.float32)
            at = block * BLOCK
            codes[chunk, :, at:at + BLOCK] = (active[:, at:at + BLOCK] * gate).astype(jnp.bfloat16)
        pl.when(layer == 0)(lambda: codes_copy(chunk).start())

    order = far_first(outer)

    def nth(place):
        value = order[0][place]
        for at in range(1, outer):
            value = jnp.where(z == at, order[at][place], value)
        return value

    def share(chunk, index, target):
        slab = index // per_slab
        columns = pl.ds(pl.multiple_of((index % per_slab) * part_cols, part_cols), part_cols)
        target[...] = jnp.dot(codes[chunk], dec_buf[slab, :, columns], preferred_element_type=jnp.float32)

        @pl.when(layer == 1)
        def _():
            target[...] += jnp.dot(early[chunk], cross_buf[slab, :, columns], preferred_element_type=jnp.float32)

    def x_copy(chunk, step, line):
        return pltpu.make_async_remote_copy(
            x_out.at[chunk, step - 1, line], x_in.at[chunk, step - 1, line],
            x_send.at[chunk, step - 1, line], x_recv.at[chunk, step - 1, line],
            device_id=to_tensor(z * inner + x_peer(step)), device_id_type=pl.DeviceIdType.MESH,
        )

    def exchange(chunk, place):
        line = nth(place)
        for step in range(1, inner):
            share(chunk, line * inner + x_peer(step), held)
            x_out[chunk, step - 1, line] = held[...].astype(jnp.bfloat16)
            x_copy(chunk, step, line).start()
        share(chunk, line * inner + x, own.at[chunk, line])

    def up_copy(chunk, line):
        return pltpu.make_async_remote_copy(
            z_out.at[chunk, line], up_in.at[chunk, line], z_send.at[chunk, line], up_recv.at[chunk, line],
            device_id=to_tensor(above), device_id_type=pl.DeviceIdType.MESH,
        )

    def down_copy(chunk, line):
        return pltpu.make_async_remote_copy(
            z_out.at[chunk, line], down_in.at[chunk, line], z_send.at[chunk, line], down_recv.at[chunk, line],
            device_id=to_tensor(below), device_id_type=pl.DeviceIdType.MESH,
        )

    def add_up(chunk, place):
        line = nth(place)
        total = own.at[chunk, line]
        for step in range(1, inner):
            x_copy(chunk, step, line).wait_recv()
            total[...] += x_in[chunk, step - 1, line].astype(jnp.float32)

        def from_below():
            up_copy(chunk, line).wait_recv()
            total[...] += up_in[chunk, line].astype(jnp.float32)

        def from_above():
            down_copy(chunk, line).wait_recv()
            total[...] += down_in[chunk, line].astype(jnp.float32)

        if place == outer - 1:
            pl.when(has_below)(from_below)
            pl.when(has_above)(from_above)
            out[0, chunk * part_rows:(chunk + 1) * part_rows, :] = total[...].astype(jnp.bfloat16)
            return

        @pl.when(line > z)
        def _():
            pl.when(has_below)(from_below)
            z_out[chunk, line] = total[...].astype(jnp.bfloat16)
            up_copy(chunk, line).start()

        @pl.when(line < z)
        def _():
            pl.when(has_above)(from_above)
            z_out[chunk, line] = total[...].astype(jnp.bfloat16)
            down_copy(chunk, line).start()

    limit_copy.wait()
    gate_copy.wait()
    weights_ready(0)
    for chunk in range(CHUNKS):
        encode(chunk)
    weights_ready(1)
    pl.when(layer == 1)(lambda: weights_ready(2))
    for chunk in range(CHUNKS):
        pl.when(layer == 1)(lambda chunk=chunk: codes_copy(chunk).wait_recv())
    sums = sorted(((c, k) for c in range(CHUNKS) for k in range(outer)), key=lambda ck: (ck[1] + SUM_LAG * ck[0], ck[0]))
    for at, item in enumerate(sums):
        exchange(*item)
        if at >= AHEAD:
            add_up(*sums[at - AHEAD])
    for item in sums[len(sums) - AHEAD:]:
        add_up(*item)

    for chunk, distance in steps:
        pass_on(chunk, distance, True)
    for which in range(3):
        for step in range(1, dp_count):
            when_used(which, lambda which=which, step=step: weight_copy(which, step).wait_send())
    for chunk in range(CHUNKS):
        pl.when(layer == 0)(lambda chunk=chunk: codes_copy(chunk).wait_send())
        for line in range(outer):
            for step in range(1, inner):
                x_copy(chunk, step, line).wait_send()
            pl.when(line > z)(lambda chunk=chunk, line=line: up_copy(chunk, line).wait_send())
            pl.when(line < z)(lambda chunk=chunk, line=line: down_copy(chunk, line).wait_send())


def shards(mesh_shape, resid_in, w_enc, threshold, block_mask, w_dec, w_cross):
    count, dp_count = mesh_shape["tensor"], mesh_shape["dp"]
    outer, inner = grid_of(count)
    _, rows, cols = resid_in.shape
    part = rows // CHUNKS
    latents = w_enc.shape[2]
    deep, wide = w_enc.shape[1], w_dec.shape[2]
    bf16, f32 = jnp.bfloat16, jnp.float32
    dma = pltpu.SemaphoreType.DMA
    vmem = pl.BlockSpec(memory_space=pltpu.VMEM)
    hbm = pl.BlockSpec(memory_space=pltpu.HBM)
    return pl.pallas_call(
        functools.partial(kernel, (outer, inner, dp_count)),
        out_shape=jax.ShapeDtypeStruct((1, rows, cols), bf16),
        in_specs=[hbm] * 6,
        out_specs=vmem,
        scratch_shapes=[
            pltpu.VMEM((1, latents), f32),
            pltpu.VMEM(block_mask.shape, jnp.int32),
            pltpu.VMEM((CHUNKS, count, part, cols), bf16),
            pltpu.VMEM((dp_count, deep, latents), bf16),
            pltpu.VMEM((dp_count, latents, wide), bf16),
            pltpu.VMEM((dp_count, latents, wide), bf16),
            pltpu.VMEM((CHUNKS, part, latents), bf16),
            pltpu.VMEM((CHUNKS, part, latents), bf16),
            pltpu.VMEM((part, cols), f32),
            pltpu.VMEM((CHUNKS, outer, part, cols), f32),
            pltpu.VMEM((CHUNKS, inner - 1, outer, part, cols), bf16),
            pltpu.VMEM((CHUNKS, inner - 1, outer, part, cols), bf16),
            pltpu.VMEM((CHUNKS, outer, part, cols), bf16),
            pltpu.VMEM((CHUNKS, outer, part, cols), bf16),
            pltpu.VMEM((CHUNKS, outer, part, cols), bf16),
            dma((2,)),
            dma((CHUNKS,)),
            dma((3,)),
            dma((3, dp_count - 1)),
            dma((3, dp_count - 1)),
            dma((CHUNKS, count)),
            dma((CHUNKS, outer, 2)),
            dma((CHUNKS, outer, inner - 1)),
            dma((CHUNKS,)),
            dma((CHUNKS,)),
            dma((CHUNKS, inner - 1, outer)),
            dma((CHUNKS, inner - 1, outer)),
            dma((CHUNKS, outer)),
            dma((CHUNKS, outer)),
            dma((CHUNKS, outer)),
        ],
        compiler_params=pltpu.CompilerParams(
            collective_id=0, has_side_effects=True, vmem_limit_bytes=60 * 1024 * 1024
        ),
        cost_estimate=pl.CostEstimate(
            flops=6 * rows * latents * cols * count, bytes_accessed=6 * deep * latents * dp_count, transcendentals=0
        ),
    )(resid_in, threshold, block_mask, w_enc[0], w_dec[0], w_cross)


def solution(mesh):
    return jax.shard_map(
        functools.partial(shards, dict(mesh.shape)),
        mesh=mesh,
        in_specs=(
            P("layer", "dp", "tensor"),
            P("layer", "dp", "tensor"),
            P("layer", "tensor"),
            P("layer", "dp", "tensor"),
            P("layer", "tensor", "dp"),
            P("tensor", "dp"),
        ),
        out_specs=P("layer", "dp", "tensor"),
        check_vma=False,
    )
```
